32 devices in a mesh: row: 4 (over x, core), col: 8 (over z, y).
Axes of the slice: x: 2, y: 2, z: 4, core: 2. Of those that a mesh axis runs over, the one named last changes fastest.
Arguments:
- gradient: bfloat16 [5120, 5120], P('row', 'col'), may hold values from -6 to 6
- left_basis: bfloat16 [5120, 5120], P('row', 'col'), may hold values from -0.078125 to 0.078125
- right_basis: bfloat16 [5120, 5120], P('row', 'col'), may hold values from -0.078125 to 0.078125
- first_moment: float32 [5120, 5120], P('row', 'col'), may hold values from -4 to 4
- second_moment: float32 [5120, 5120], P('row', 'col'), may hold values from 0.05 to 2
Outputs:
- update: bfloat16 [5120, 5120], P('row', 'col')
- new_first: float32 [5120, 5120], P('row', 'col')
- new_second: float32 [5120, 5120], P('row', 'col')
The draws below stay inside these ranges and needn't reach their ends.
All inputs are finite; a program needn't handle non-finite values.
Results may differ from the reference program's by a relative error of at most 0.006.
Values may be sent and summed in bfloat16 or wider, within the bound.
A program may use at most 192 MiB of HBM per device.

```python
import math
import jax
import jax.numpy as jnp

M = 5120
STEP = 10


def block_scale(stream_key, shape, split, least, top_value):
    level = 1.0
    for dim, blocks in split:
        draws = jax.random.uniform(jax.random.fold_in(jax.random.fold_in(stream_key, 6), dim), (blocks,), jnp.float32, least / len(split), top_value / len(split))
        level = level * jnp.repeat(jnp.exp(draws), shape[dim] // blocks).reshape((-1,) + (1,) * (len(shape) - 1 - dim))
    return level


def normal_values(key, shape, spread, limit, split=(), dtype=jnp.bfloat16):
    level = block_scale(key, shape, split, -0.22, 0.18) if split else 1.0
    array = jax.random.normal(key, shape, jnp.float32) * spread * level
    return jnp.minimum(jnp.maximum(array, -limit), limit).astype(dtype)


def setup_inputs(seed: int = 0) -> dict:
    streams_of = jax.random.split(jax.random.key(seed), 6)
    gradient = normal_values(streams_of[0], (M, M), 1.0, 6.0, ((0, 4), (1, 8)))
    left_basis = normal_values(streams_of[1], (M, M), M ** -0.5, 0.078125, ((0, 4), (1, 8)))
    right_basis = normal_values(streams_of[2], (M, M), M ** -0.5, 0.078125, ((0, 4), (1, 8)))
    first_moment = normal_values(streams_of[3], (M, M), 0.3, 4.0, ((0, 4), (1, 8)), jnp.float32)
    second_moment = jnp.clip(jnp.exp(math.log(2.0) - 3.6888794 * jax.random.uniform(streams_of[4], (M, M), jnp.float32) ** block_scale(streams_of[4], (M, M), ((0, 4), (1, 8)), -0.2, 0.2)), 0.05, 2.0)
    return dict(gradient=gradient, left_basis=left_basis, right_basis=right_basis, first_moment=first_moment, second_moment=second_moment)


def reference(gradient, left_basis, right_basis, first_moment, second_moment):
    left_rotated = jnp.dot(left_basis.T, gradient, preferred_element_type=jnp.float32).astype(jnp.bfloat16)
    rotated = jnp.dot(left_rotated, right_basis, preferred_element_type=jnp.float32)
    new_first = 0.9 * first_moment + 0.1 * rotated
    new_second = 0.95 * second_moment + 0.05 * rotated * rotated
    first_fix = 1.0 - 0.9 ** STEP
    second_fix = 1.0 - 0.95 ** STEP
    direction = (new_first / first_fix / (jnp.sqrt(new_second / second_fix) + 1e-08)).astype(jnp.bfloat16)
    back_left = jnp.dot(left_basis, direction, preferred_element_type=jnp.float32).astype(jnp.bfloat16)
    update = jnp.dot(back_left, right_basis.T, preferred_element_type=jnp.float32).astype(jnp.bfloat16)
    return (update, new_first, new_second)
```

```python
import jax
import jax.numpy as jnp
from jax import lax
from jax.sharding import PartitionSpec as P

STEP = 10


def body(gradient, left_basis, right_basis, first_moment, second_moment):
    left_panel = lax.all_gather(left_basis, "col", axis=1, tiled=True)
    right_panel = lax.all_gather(right_basis, "row", axis=0, tiled=True)
    columns = left_panel
    left_rotated = lax.psum_scatter(
        lax.dot_general(
            columns, gradient, (((0,), (0,)), ((), ())), preferred_element_type=jnp.float32
        ).astype(jnp.bfloat16),
        "row",
        scatter_dimension=0,
        tiled=True,
    ).astype(jnp.bfloat16)
    rotated = jnp.dot(
        lax.all_gather(left_rotated, "col", axis=1, tiled=True),
        right_panel,
        preferred_element_type=jnp.float32,
    )
    new_first = 0.9 * first_moment + 0.1 * rotated
    new_second = 0.95 * second_moment + 0.05 * rotated * rotated
    first_fix = 1.0 - 0.9**STEP
    second_fix = 1.0 - 0.95**STEP
    direction = (new_first / first_fix / (jnp.sqrt(new_second / second_fix) + 1e-08)).astype(
        jnp.bfloat16
    )
    columns = left_panel
    back_left = jnp.dot(
        columns,
        lax.all_gather(direction, "row", axis=0, tiled=True),
        preferred_element_type=jnp.float32,
    ).astype(jnp.bfloat16)
    partial_terms = lax.dot_general(
        back_left, right_panel, (((1,), (1,)), ((), ())), preferred_element_type=jnp.float32
    )
    update = lax.psum_scatter(partial_terms.astype(jnp.bfloat16), "col", scatter_dimension=1, tiled=True)
    return (update.astype(jnp.bfloat16), new_first, new_second)


def solution(mesh):
    placed = (P("row", "col"), P("row", "col"), P("row", "col"), P("row", "col"), P("row", "col"))
    return jax.shard_map(
        body,
        mesh=mesh,
        in_specs=placed,
        out_specs=(P("row", "col"), P("row", "col"), P("row", "col")),
        check_vma=False,
    )
```

```python
import functools
import jax
import jax.numpy as jnp
from jax import lax
from jax.experimental import pallas as pl
from jax.experimental.pallas import tpu as pltpu
from jax.sharding import PartitionSpec as P

STEP = 10
LINE = 4
MESH = pl.DeviceIdType.MESH
BF16 = jnp.bfloat16
F32 = jnp.float32


def tile_of(size, wanted):
    return wanted if size % wanted == 0 else size


class Place:
    def __init__(self, rows, cols):
        self.rows, self.cols = rows, cols
        self.breadth = cols // LINE
        self.r, self.c = lax.axis_index("row"), lax.axis_index("col")
        self.a, self.b = self.c // self.breadth, self.c % self.breadth

    def beside(self, k):
        return (self.b + k) % self.breadth

    def row_peer(self, k):
        return (self.r + k) % self.rows

    def greet(self, across, along):
        barrier = pltpu.get_barrier_semaphore()

        def hello(row, col):
            pl.semaphore_signal(barrier, inc=1, device_id=(row, col), device_id_type=MESH)

        count = 0
        if along:
            for k in range(1, self.breadth):
                hello(self.r, self.a * self.breadth + self.beside(k))
                count += 1

            @pl.when(self.a > 0)
            def _():
                hello(self.r, self.c - self.breadth)

            @pl.when(self.a < LINE - 1)
            def _():
                hello(self.r, self.c + self.breadth)

        if across:
            for k in range(1, self.rows):
                hello(self.row_peer(k), self.c)
                count += 1
        if not along:
            pl.semaphore_wait(barrier, count)
            return
        end = (self.a == 0) | (self.a == LINE - 1)

        @pl.when(end)
        def _():
            pl.semaphore_wait(barrier, count + 1)

        @pl.when(jnp.logical_not(end))
        def _():
            pl.semaphore_wait(barrier, count + 2)


def remote(src, dst, send, recv, row, col):
    return pltpu.make_async_remote_copy(
        src_ref=src,
        dst_ref=dst,
        send_sem=send,
        recv_sem=recv,
        device_id=(row, col),
        device_id_type=MESH,
    )


def gather_along(at, panel, send, recv, process, between=None):
    a, b, B = at.a, at.b, at.breadth

    def right(slot):
        return remote(panel.at[slot], panel.at[slot], send.at[0, slot], recv.at[slot], at.r, at.c + B)

    def left(slot):
        return remote(panel.at[slot], panel.at[slot], send.at[1, slot], recv.at[slot], at.r, at.c - B)

    def over(slot, k):
        return remote(panel.at[slot], panel.at[slot], send.at[1 + k, slot], recv.at[slot], at.r, a * B + at.beside(k))

    def arrived(slot):
        remote(panel.at[slot], panel.at[slot], send.at[0, slot], recv.at[slot], at.r, at.c).wait_recv()

    @pl.when(a < LINE - 1)
    def _():
        right(at.c).start()

    @pl.when(a > 0)
    def _():
        left(at.c).start()

    for k in range(1, B):
        over(at.c, k).start()
    process(at.c)

    def beside(s):
        for sign in (-1, 1) if s else (1,):
            far = a + sign * s

            @pl.when((far >= 0) & (far < LINE))
            def _():
                for k in range(1, B):
                    slot = far * B + at.beside(k)
                    arrived(slot)
                    process(slot)

    for s in range(1, LINE):

        @pl.when(a - s >= 0)
        def _():
            slot = (a - s) * B + b
            arrived(slot)

            @pl.when(a < LINE - 1)
            def _():
                right(slot).start()

            for k in range(1, B):
                over(slot, k).start()

        @pl.when(a + s < LINE)
        def _():
            slot = (a + s) * B + b
            arrived(slot)

            @pl.when(a > 0)
            def _():
                left(slot).start()

            for k in range(1, B):
                over(slot, k).start()

        if between is not None and s == 1:
            between()
        for sign in (-1, 1):
            far = a + sign * s

            @pl.when((far >= 0) & (far < LINE))
            def _():
                process(far * B + b)

        beside(s - 1)
    beside(LINE - 1)

    def drain():
        for s in range(LINE):

            @pl.when((a - s >= 0) & (a < LINE - 1))
            def _():
                right((a - s) * B + b).wait_send()

            @pl.when((a + s < LINE) & (a > 0))
            def _():
                left((a + s) * B + b).wait_send()

        for s in range(LINE):
            for k in range(1, B):
                over(s * B + b, k).wait_send()

    return drain


class Across:
    def __init__(self, at, panel, send, recv):
        self.at, self.panel, self.send, self.recv = at, panel, send, recv
        self.chips = at.rows // 2
        self.core, self.chip = at.r % 2, at.r // 2
        self.sibling = self.chip * 2 + 1 - self.core

    def far(self, k):
        return ((self.chip + k) % self.chips) * 2 + self.core

    def far_pair(self, k):
        return ((self.chip + k) % self.chips) * 2 + 1 - self.core

    def go(self, slot, lane, row):
        ref = self.panel.at[slot]
        return remote(ref, ref, self.send.at[lane, slot], self.recv.at[slot], row, self.at.c)

    def arrived(self, slot):
        self.go(slot, 0, self.at.r).wait_recv()

    def start(self):
        for k in range(1, self.chips):
            self.go(self.at.r, k, self.far(k)).start()
        self.go(self.at.r, 0, self.sibling).start()

    def forward(self, process=None):
        for k in range(1, self.chips):
            slot = self.far(self.chips - k)
            self.arrived(slot)
            self.go(slot, 0, self.sibling).start()
            if process is not None:
                process(slot)

    def finish(self, process=None):
        self.arrived(self.sibling)
        if process is not None:
            process(self.sibling)
        for k in range(1, self.chips):
            slot = self.far_pair(k)
            self.arrived(slot)
            if process is not None:
                process(slot)

    def drain(self):
        for k in range(1, self.chips):
            self.go(self.at.r, k, self.far(k)).wait_send()
            self.go(self.far(k), 0, self.sibling).wait_send()
        self.go(self.at.r, 0, self.sibling).wait_send()


def first_kernel(
    rows, cols, left, grad, right, lpanel, rpanel, out, stage, partial, lsend, lrecv, rsend, rrecv, psend, precv
):
    at = Place(rows, cols)
    q = cols // rows
    n = left.shape[1]
    tile = tile_of(n, 128)
    at.greet(True, True)
    lpanel[at.c] = left[...]
    rpanel[at.r] = right[...]
    across = Across(at, rpanel, rsend, rrecv)
    across.start()

    def send(slot):
        to, t = slot // q, slot % q
        return remote(stage.at[slot], partial.at[at.r, t], psend.at[slot], precv.at[at.r, t], to, at.c)

    def process(slot):
        def step(i, _):
            span = pl.ds(pl.multiple_of(i * tile, tile), tile)
            stage[slot, span, :] = lax.dot_general(
                lpanel[slot, :, span], grad[...], (((0,), (0,)), ((), ())), preferred_element_type=F32
            ).astype(BF16)
            return 0

        lax.fori_loop(0, n // tile, step, 0)

        @pl.when(slot // q != at.r)
        def _():
            send(slot).start()

    drain = gather_along(at, lpanel, lsend, lrecv, process, across.forward)
    across.finish()
    for k in range(1, rows):
        for t in range(q):
            src = at.row_peer(k)
            ref = partial.at[src, t]
            remote(ref, ref, psend.at[0], precv.at[src, t], at.r, at.c).wait_recv()
    part = tile_of(n, 64)
    for t in range(q):

        def add(i, _):
            span = pl.ds(pl.multiple_of(i * part, part), part)
            total = stage[at.r * q + t, span, :].astype(F32)
            for k in range(1, rows):
                total += partial[at.row_peer(k), t, span, :].astype(F32)
            out[pl.ds(pl.multiple_of(t * n + i * part, part), part), :] = total.astype(BF16)
            return 0

        lax.fori_loop(0, n // part, add, 0)
    for k in range(1, rows):
        for t in range(q):
            send(at.row_peer(k) * q + t).wait_send()
    drain()
    across.drain()


def second_kernel(rows, cols, lr, rpanel, out, panel, send, recv):
    at = Place(rows, cols)
    q = cols // rows
    m, n = lr.shape
    tile = tile_of(m, 256) if m % 256 == 0 else tile_of(m, 128)
    at.greet(False, True)
    panel[at.c] = lr[...]
    out[...] = jnp.zeros_like(out)

    def process(slot):
        to, t = slot // q, slot % q
        depth = pl.ds(pl.multiple_of(t * n, n), n)

        def step(i, _):
            span = pl.ds(pl.multiple_of(i * tile, tile), tile)
            out[span, :] += jnp.dot(panel[slot, span, :], rpanel[to, depth, :], preferred_element_type=F32)
            return 0

        lax.fori_loop(0, m // tile, step, 0)

    gather_along(at, panel, send, recv, process)()


def third_kernel(
    rows, cols, parts, d, lpanel, rpanel, out, dpanel, total, back, near, line, dsend, drecv, nsend, nrecv, zsend, zrecv
):
    at = Place(rows, cols)
    a, B = at.a, at.breadth
    q = cols // rows
    m, n = d.shape
    tile = tile_of(m, 256) if m % 256 == 0 else tile_of(m, 128)
    high = m // parts
    fine = tile_of(high, 128)
    at.greet(True, True)
    dpanel[at.r] = d[...]
    across = Across(at, dpanel, dsend, drecv)
    across.start()
    total[...] = jnp.zeros_like(total)

    def gain(slot):
        def step(i, _):
            span = pl.ds(pl.multiple_of(i * tile, tile), tile)
            value = total[span, :]
            for t in range(q):
                value += jnp.dot(
                    lpanel[slot * q + t, span, :], dpanel[slot, t * n : (t + 1) * n, :], preferred_element_type=F32
                )
            total[span, :] = value
            return 0

        lax.fori_loop(0, m // tile, step, 0)

    gain(at.r)
    across.forward(gain)
    across.finish(gain)
    back[...] = total[...].astype(BF16)

    def over(k, target, h):
        rows_of = pl.ds(h * high, high)
        return remote(
            near.at[k - 1, 0, target, rows_of],
            near.at[k - 1, 1, target, rows_of],
            nsend.at[k - 1, target, h],
            nrecv.at[k - 1, target, h],
            at.r,
            a * B + at.beside(k),
        )

    def term(i, col):
        to, t = col // q, col % q
        return lax.dot_general(
            back[pl.ds(pl.multiple_of(i, fine), fine), :],
            rpanel[to, pl.ds(pl.multiple_of(t * n, n), n), :],
            (((1,), (1,)), ((), ())),
            preferred_element_type=F32,
        )

    order = []
    low, top = 0, LINE - 1
    while low <= top:
        order += [top, low] if low < top else [low]
        low, top = low + 1, top - 1
    pieces = [(target, h) for target in order for h in range(parts)]
    for target, h in pieces:
        for k in range(1, B):

            def fill(i, _):
                at_row = h * high + i * fine
                near[k - 1, 0, target, pl.ds(pl.multiple_of(at_row, fine), fine), :] = term(
                    at_row, target * B + at.beside(k)
                ).astype(BF16)
                return 0

            lax.fori_loop(0, high // fine, fill, 0)
            over(k, target, h).start()

    def shift(target, h, step):
        rows_of = pl.ds(h * high, high)
        slot = target if step > 0 else jnp.where(a - 1 == target, LINE, target)
        return remote(
            near.at[0, 1, target, rows_of],
            line.at[slot, rows_of],
            zsend.at[target, h],
            zrecv.at[slot, h],
            at.r,
            at.c + step * B,
        )

    def landed(slot, h):
        ref = line.at[slot, pl.ds(h * high, high)]
        remote(ref, ref, zsend.at[0, h], zrecv.at[slot, h], at.r, at.c).wait_recv()

    for target, h in pieces:
        for k in range(1, B):
            over(k, target, h).wait_recv()

        def combine(extra):
            def add(i, _):
                at_row = h * high + i * fine
                span = pl.ds(pl.multiple_of(at_row, fine), fine)
                value = term(at_row, target * B + at.b)
                for k in range(1, B):
                    value += near[k - 1, 1, target, span, :].astype(F32)
                if extra:
                    value += line[target, span, :].astype(F32)
                near[0, 1, target, span, :] = value.astype(BF16)
                return 0

            lax.fori_loop(0, high // fine, add, 0)

        def alone():
            combine(False)

        def joined():
            landed(target, h)
            combine(True)

        if target > 0:

            @pl.when(a == 0)
            def _():
                alone()
                shift(target, h, 1).start()

            @pl.when((a > 0) & (a < target))
            def _():
                joined()
                shift(target, h, 1).start()

        if target < LINE - 1:

            @pl.when(a == LINE - 1)
            def _():
                alone()
                shift(target, h, -1).start()

            @pl.when((a < LINE - 1) & (a > target))
            def _():
                joined()
                shift(target, h, -1).start()

        @pl.when(a == target)
        def _():
            alone()

    for h in range(parts):

        @pl.when(a > 0)
        def _():
            landed(a, h)

        @pl.when(a < LINE - 1)
        def _():
            landed(LINE, h)

        def last(use_left, use_right):
            def add(i, _):
                span = pl.ds(pl.multiple_of(h * high + i * fine, fine), fine)
                value = near[0, 1, a, span, :].astype(F32)
                if use_left:
                    value += line[a, span, :].astype(F32)
                if use_right:
                    value += line[LINE, span, :].astype(F32)
                out[span, :] = value.astype(BF16)
                return 0

            lax.fori_loop(0, high // fine, add, 0)

        pl.when(a == 0)(functools.partial(last, False, True))
        pl.when(a == LINE - 1)(functools.partial(last, True, False))
        pl.when((a > 0) & (a < LINE - 1))(functools.partial(last, True, True))

    for target, h in pieces:
        for k in range(1, B):
            over(k, target, h).wait_send()

        @pl.when(a != target)
        def _():
            shift(target, h, 1).wait_send()

    across.drain()


def call(kernel, number, outs, ins, scratch, flops):
    vmem = pl.BlockSpec(memory_space=pltpu.VMEM)
    return pl.pallas_call(
        kernel,
        out_shape=outs,
        in_specs=[vmem] * ins,
        out_specs=jax.tree.map(lambda _: vmem, outs),
        scratch_shapes=scratch,
        compiler_params=pltpu.CompilerParams(
            collective_id=number, has_side_effects=True, vmem_limit_bytes=60 * 1024 * 1024
        ),
        cost_estimate=pl.CostEstimate(flops=flops, bytes_accessed=30_000_000, transcendentals=0),
    )


def body(rows, cols, gradient, left_basis, right_basis, first_moment, second_moment):
    m, n = gradient.shape
    q = cols // rows
    B = cols // LINE
    dma = pltpu.SemaphoreType.DMA
    shape = jax.ShapeDtypeStruct
    flops = 2 * m * n * m * rows
    chips = rows // 2
    lpanel, rpanel, left_rotated = call(
        functools.partial(first_kernel, rows, cols),
        0,
        (shape((cols, m, n), BF16), shape((rows, m, n), BF16), shape((m, n), BF16)),
        3,
        [
            pltpu.VMEM((cols, n, n), BF16),
            pltpu.VMEM((rows, q, n, n), BF16),
            dma((1 + B, cols)),
            dma((cols,)),
            dma((chips, rows)),
            dma((rows,)),
            dma((cols,)),
            dma((rows, q)),
        ],
        flops,
    )(left_basis, gradient, right_basis)
    rotated = call(
        functools.partial(second_kernel, rows, cols),
        1,
        shape((m, n), F32),
        2,
        [pltpu.VMEM((cols, m, n), BF16), dma((1 + B, cols)), dma((cols,))],
        flops,
    )(left_rotated, rpanel)
    new_first = 0.9 * first_moment + 0.1 * rotated
    new_second = 0.95 * second_moment + 0.05 * rotated * rotated
    first_fix = 1.0 - 0.9**STEP
    second_fix = 1.0 - 0.95**STEP
    direction = (new_first / first_fix / (jnp.sqrt(new_second / second_fix) + 1e-08)).astype(BF16)
    parts = 2
    update = call(
        functools.partial(third_kernel, rows, cols, parts),
        2,
        shape((m, n), BF16),
        3,
        [
            pltpu.VMEM((rows, m, n), BF16),
            pltpu.VMEM((m, n), F32),
            pltpu.VMEM((m, n), BF16),
            pltpu.VMEM((B - 1, 2, LINE, m, n), BF16),
            pltpu.VMEM((LINE + 1, m, n), BF16),
            dma((chips, rows)),
            dma((rows,)),
            dma((B - 1, LINE, parts)),
            dma((B - 1, LINE, parts)),
            dma((LINE, parts)),
            dma((LINE + 1, parts)),
        ],
        2 * flops,
    )(direction, lpanel, rpanel)
    return (update, new_first, new_second)


def solution(mesh):
    spec = P("row", "col")
    return jax.shard_map(
        functools.partial(body, mesh.shape["row"], mesh.shape["col"]),
        mesh=mesh,
        in_specs=(spec,) * 5,
        out_specs=(spec,) * 3,
        check_vma=False,
    )
```

```python
import functools
import jax
import jax.numpy as jnp
from jax import lax
from jax.experimental import pallas as pl
from jax.experimental.pallas import tpu as pltpu
from jax.sharding import PartitionSpec as P

STEP = 10
LINE = 4
MESH = pl.DeviceIdType.MESH
BF16 = jnp.bfloat16
F32 = jnp.float32


def tile_of(size, wanted):
    return wanted if size % wanted == 0 else size


class Place:
    def __init__(self, rows, cols):
        self.rows, self.cols = rows, cols
        self.breadth = cols // LINE
        self.r, self.c = lax.axis_index("row"), lax.axis_index("col")
        self.a, self.b = self.c // self.breadth, self.c % self.breadth

    def beside(self, k):
        return (self.b + k) % self.breadth

    def row_peer(self, k):
        return (self.r + k) % self.rows

    def greet(self, across, along):
        barrier = pltpu.get_barrier_semaphore()

        def hello(row, col):
            pl.semaphore_signal(barrier, inc=1, device_id=(row, col), device_id_type=MESH)

        count = 0
        if along:
            for k in range(1, self.breadth):
                hello(self.r, self.a * self.breadth + self.beside(k))
                count += 1

            @pl.when(self.a > 0)
            def _():
                hello(self.r, self.c - self.breadth)

            @pl.when(self.a < LINE - 1)
            def _():
                hello(self.r, self.c + self.breadth)

        if across:
            for k in range(1, self.rows):
                hello(self.row_peer(k), self.c)
                count += 1
        if not along:
            pl.semaphore_wait(barrier, count)
            return
        end = (self.a == 0) | (self.a == LINE - 1)

        @pl.when(end)
        def _():
            pl.semaphore_wait(barrier, count + 1)

        @pl.when(jnp.logical_not(end))
        def _():
            pl.semaphore_wait(barrier, count + 2)


def remote(src, dst, send, recv, row, col):
    return pltpu.make_async_remote_copy(
        src_ref=src,
        dst_ref=dst,
        send_sem=send,
        recv_sem=recv,
        device_id=(row, col),
        device_id_type=MESH,
    )


def gather_along(at, panel, send, recv, process, between=None):
    a, b, B = at.a, at.b, at.breadth

    def right(slot):
        return remote(panel.at[slot], panel.at[slot], send.at[0, slot], recv.at[slot], at.r, at.c + B)

    def left(slot):
        return remote(panel.at[slot], panel.at[slot], send.at[1, slot], recv.at[slot], at.r, at.c - B)

    def over(slot, k):
        return remote(panel.at[slot], panel.at[slot], send.at[1 + k, slot], recv.at[slot], at.r, a * B + at.beside(k))

    def arrived(slot):
        remote(panel.at[slot], panel.at[slot], send.at[0, slot], recv.at[slot], at.r, at.c).wait_recv()

    half = panel.shape[1] // 2
    mate = a + 1 - 2 * (a % 2)

    def over_half(slot, k):
        ref = panel.at[slot, pl.ds(0, half)]
        return remote(ref, ref, send.at[1 + k, slot], recv.at[slot], at.r, a * B + at.beside(k))

    def to_mate(slot):
        ref = panel.at[slot, pl.ds(half, half)]
        return remote(ref, ref, send.at[0, slot], recv.at[LINE * B + slot], at.r, mate * B + b)

    def arrived_halves(slot):
        for h in range(2):
            ref = panel.at[slot, pl.ds(h * half, half)]
            remote(ref, ref, send.at[0, slot], recv.at[h * LINE * B + slot], at.r, at.c).wait_recv()

    def sides(far, start):
        for k in range(1, B):

            @pl.when(far == mate)
            def _():
                start(over_half(far * B + b, k))

            @pl.when(far != mate)
            def _():
                start(over(far * B + b, k))

    def begin(copy):
        copy.start()

    def leave(copy):
        copy.wait_send()

    @pl.when(a < LINE - 1)
    def _():
        right(at.c).start()

    @pl.when(a > 0)
    def _():
        left(at.c).start()

    for k in range(1, B):
        over(at.c, k).start()
    process(at.c)

    def beside(s):
        for sign in (-1, 1) if s else (1,):
            far = a + sign * s

            @pl.when((far >= 0) & (far < LINE))
            def _():
                for k in range(1, B):
                    slot = far * B + at.beside(k)
                    if s == 1:
                        pl.when(far == mate)(functools.partial(arrived_halves, slot))
                        pl.when(far != mate)(functools.partial(arrived, slot))
                    else:
                        arrived(slot)
                    if s == 0:
                        to_mate(slot).start()
                    process(slot)

    for s in range(1, LINE):

        @pl.when(a - s >= 0)
        def _():
            slot = (a - s) * B + b
            arrived(slot)

            @pl.when(a < LINE - 1)
            def _():
                right(slot).start()

            sides(a - s, begin)

        @pl.when(a + s < LINE)
        def _():
            slot = (a + s) * B + b
            arrived(slot)

            @pl.when(a > 0)
            def _():
                left(slot).start()

            sides(a + s, begin)

        if between is not None and s == LINE - 2:
            between()
        for sign in (-1, 1):
            far = a + sign * s

            @pl.when((far >= 0) & (far < LINE))
            def _():
                process(far * B + b)

        beside(s - 1)
    beside(LINE - 1)

    def drain():
        for s in range(LINE):

            @pl.when((a - s >= 0) & (a < LINE - 1))
            def _():
                right((a - s) * B + b).wait_send()

            @pl.when((a + s < LINE) & (a > 0))
            def _():
                left((a + s) * B + b).wait_send()

        for s in range(LINE):
            sides(s, leave)
        for k in range(1, B):
            to_mate(a * B + at.beside(k)).wait_send()

    return drain


class Across:
    def __init__(self, at, panel, send, recv):
        self.at, self.panel, self.send, self.recv = at, panel, send, recv
        self.chips = at.rows // 2
        self.core, self.chip = at.r % 2, at.r // 2
        self.sibling = self.chip * 2 + 1 - self.core

    def far(self, k):
        return ((self.chip + k) % self.chips) * 2 + self.core

    def far_pair(self, k):
        return ((self.chip + k) % self.chips) * 2 + 1 - self.core

    def go(self, slot, lane, row):
        ref = self.panel.at[slot]
        return remote(ref, ref, self.send.at[lane, slot], self.recv.at[slot], row, self.at.c)

    def arrived(self, slot):
        self.go(slot, 0, self.at.r).wait_recv()

    def start(self):
        for k in range(1, self.chips):
            self.go(self.at.r, k, self.far(k)).start()
        self.go(self.at.r, 0, self.sibling).start()

    def forward(self, process=None):
        for k in range(1, self.chips):
            slot = self.far(self.chips - k)
            self.arrived(slot)
            self.go(slot, 0, self.sibling).start()
            if process is not None:
                process(slot)

    def finish(self, process=None):
        self.arrived(self.sibling)
        if process is not None:
            process(self.sibling)
        for k in range(1, self.chips):
            slot = self.far_pair(k)
            self.arrived(slot)
            if process is not None:
                process(slot)

    def drain(self):
        for k in range(1, self.chips):
            self.go(self.at.r, k, self.far(k)).wait_send()
            self.go(self.far(k), 0, self.sibling).wait_send()
        self.go(self.at.r, 0, self.sibling).wait_send()


def first_kernel(
    rows, cols, left, grad, right, lpanel, rpanel, out, stage, partial, lsend, lrecv, rsend, rrecv, psend, precv
):
    at = Place(rows, cols)
    q = cols // rows
    n = left.shape[1]
    tile = tile_of(n, 128)
    at.greet(True, True)
    lpanel[at.c] = left[...]
    rpanel[at.r] = right[...]
    across = Across(at, rpanel, rsend, rrecv)
    across.start()

    def send(slot):
        to, t = slot // q, slot % q
        return remote(stage.at[slot], partial.at[at.r, t], psend.at[slot], precv.at[at.r, t], to, at.c)

    def process(slot):
        def step(i, _):
            span = pl.ds(pl.multiple_of(i * tile, tile), tile)
            stage[slot, span, :] = lax.dot_general(
                lpanel[slot, :, span], grad[...], (((0,), (0,)), ((), ())), preferred_element_type=F32
            ).astype(BF16)
            return 0

        lax.fori_loop(0, n // tile, step, 0)

        @pl.when(slot // q != at.r)
        def _():
            send(slot).start()

    drain = gather_along(at, lpanel, lsend, lrecv, process, across.forward)
    across.finish()
    for k in range(1, rows):
        for t in range(q):
            src = at.row_peer(k)
            ref = partial.at[src, t]
            remote(ref, ref, psend.at[0], precv.at[src, t], at.r, at.c).wait_recv()
    part = tile_of(n, 64)
    for t in range(q):

        def add(i, _):
            span = pl.ds(pl.multiple_of(i * part, part), part)
            total = stage[at.r * q + t, span, :].astype(F32)
            for k in range(1, rows):
                total += partial[at.row_peer(k), t, span, :].astype(F32)
            out[pl.ds(pl.multiple_of(t * n + i * part, part), part), :] = total.astype(BF16)
            return 0

        lax.fori_loop(0, n // part, add, 0)
    for k in range(1, rows):
        for t in range(q):
            send(at.row_peer(k) * q + t).wait_send()
    drain()
    across.drain()


def second_kernel(rows, cols, lr, rpanel, out, panel, send, recv):
    at = Place(rows, cols)
    q = cols // rows
    m, n = lr.shape
    tile = tile_of(m, 256) if m % 256 == 0 else tile_of(m, 128)
    at.greet(False, True)
    panel[at.c] = lr[...]
    out[...] = jnp.zeros_like(out)

    def process(slot):
        to, t = slot // q, slot % q
        depth = pl.ds(pl.multiple_of(t * n, n), n)

        def step(i, _):
            span = pl.ds(pl.multiple_of(i * tile, tile), tile)
            out[span, :] += jnp.dot(panel[slot, span, :], rpanel[to, depth, :], preferred_element_type=F32)
            return 0

        lax.fori_loop(0, m // tile, step, 0)

    gather_along(at, panel, send, recv, process)()


def third_kernel(
    rows, cols, parts, d, lpanel, rpanel, out, dpanel, total, back, near, line, dsend, drecv, nsend, nrecv, zsend, zrecv
):
    at = Place(rows, cols)
    a, B = at.a, at.breadth
    q = cols // rows
    m, n = d.shape
    tile = tile_of(m, 256) if m % 256 == 0 else tile_of(m, 128)
    high = m // parts
    fine = tile_of(high, 128)
    at.greet(True, True)
    dpanel[at.r] = d[...]
    across = Across(at, dpanel, dsend, drecv)
    across.start()
    total[...] = jnp.zeros_like(total)

    def gain(slot):
        def step(i, _):
            span = pl.ds(pl.multiple_of(i * tile, tile), tile)
            value = total[span, :]
            for t in range(q):
                value += jnp.dot(
                    lpanel[slot * q + t, span, :], dpanel[slot, t * n : (t + 1) * n, :], preferred_element_type=F32
                )
            total[span, :] = value
            return 0

        lax.fori_loop(0, m // tile, step, 0)

    gain(at.r)
    across.forward(gain)
    across.finish(gain)
    back[...] = total[...].astype(BF16)

    def over(k, target, h):
        rows_of = pl.ds(h * high, high)
        return remote(
            near.at[k - 1, 0, target, rows_of],
            near.at[k - 1, 1, target, rows_of],
            nsend.at[k - 1, target, h],
            nrecv.at[k - 1, target, h],
            at.r,
            a * B + at.beside(k),
        )

    def term(i, col):
        to, t = col // q, col % q
        return lax.dot_general(
            back[pl.ds(pl.multiple_of(i, fine), fine), :],
            rpanel[to, pl.ds(pl.multiple_of(t * n, n), n), :],
            (((1,), (1,)), ((), ())),
            preferred_element_type=F32,
        )

    order = []
    low, top = 0, LINE - 1
    while low <= top:
        order += [top, low] if low < top else [low]
        low, top = low + 1, top - 1
    pieces = [(target, h) for target in order for h in range(parts)]
    for target, h in pieces:
        for k in range(1, B):

            def fill(i, _):
                at_row = h * high + i * fine
                near[k - 1, 0, target, pl.ds(pl.multiple_of(at_row, fine), fine), :] = term(
                    at_row, target * B + at.beside(k)
                ).astype(BF16)
                return 0

            lax.fori_loop(0, high // fine, fill, 0)
            over(k, target, h).start()

    def shift(target, h, step):
        rows_of = pl.ds(h * high, high)
        slot = target if step > 0 else jnp.where(a - 1 == target, LINE, target)
        return remote(
            near.at[0, 1, target, rows_of],
            line.at[slot, rows_of],
            zsend.at[target, h],
            zrecv.at[slot, h],
            at.r,
            at.c + step * B,
        )

    def landed(slot, h):
        ref = line.at[slot, pl.ds(h * high, high)]
        remote(ref, ref, zsend.at[0, h], zrecv.at[slot, h], at.r, at.c).wait_recv()

    for target, h in pieces:
        for k in range(1, B):
            over(k, target, h).wait_recv()

        def combine(extra):
            def add(i, _):
                at_row = h * high + i * fine
                span = pl.ds(pl.multiple_of(at_row, fine), fine)
                value = term(at_row, target * B + at.b)
                for k in range(1, B):
                    value += near[k - 1, 1, target, span, :].astype(F32)
                if extra:
                    value += line[target, span, :].astype(F32)
                near[0, 1, target, span, :] = value.astype(BF16)
                return 0

            lax.fori_loop(0, high // fine, add, 0)

        def alone():
            combine(False)

        def joined():
            landed(target, h)
            combine(True)

        if target > 0:

            @pl.when(a == 0)
            def _():
                alone()
                shift(target, h, 1).start()

            @pl.when((a > 0) & (a < target))
            def _():
                joined()
                shift(target, h, 1).start()

        if target < LINE - 1:

            @pl.when(a == LINE - 1)
            def _():
                alone()
                shift(target, h, -1).start()

            @pl.when((a < LINE - 1) & (a > target))
            def _():
                joined()
                shift(target, h, -1).start()

        @pl.when(a == target)
        def _():
            alone()

    for h in range(parts):

        @pl.when(a > 0)
        def _():
            landed(a, h)

        @pl.when(a < LINE - 1)
        def _():
            landed(LINE, h)

        def last(use_left, use_right):
            def add(i, _):
                span = pl.ds(pl.multiple_of(h * high + i * fine, fine), fine)
                value = near[0, 1, a, span, :].astype(F32)
                if use_left:
                    value += line[a, span, :].astype(F32)
                if use_right:
                    value += line[LINE, span, :].astype(F32)
                out[span, :] = value.astype(BF16)
                return 0

            lax.fori_loop(0, high // fine, add, 0)

        pl.when(a == 0)(functools.partial(last, False, True))
        pl.when(a == LINE - 1)(functools.partial(last, True, False))
        pl.when((a > 0) & (a < LINE - 1))(functools.partial(last, True, True))

    for target, h in pieces:
        for k in range(1, B):
            over(k, target, h).wait_send()

        @pl.when(a != target)
        def _():
            shift(target, h, 1).wait_send()

    across.drain()


def call(kernel, number, outs, ins, scratch, flops):
    vmem = pl.BlockSpec(memory_space=pltpu.VMEM)
    return pl.pallas_call(
        kernel,
        out_shape=outs,
        in_specs=[vmem] * ins,
        out_specs=jax.tree.map(lambda _: vmem, outs),
        scratch_shapes=scratch,
        compiler_params=pltpu.CompilerParams(
            collective_id=number, has_side_effects=True, vmem_limit_bytes=60 * 1024 * 1024
        ),
        cost_estimate=pl.CostEstimate(flops=flops, bytes_accessed=30_000_000, transcendentals=0),
    )


def body(rows, cols, gradient, left_basis, right_basis, first_moment, second_moment):
    m, n = gradient.shape
    q = cols // rows
    B = cols // LINE
    dma = pltpu.SemaphoreType.DMA
    shape = jax.ShapeDtypeStruct
    flops = 2 * m * n * m * rows
    chips = rows // 2
    lpanel, rpanel, left_rotated = call(
        functools.partial(first_kernel, rows, cols),
        0,
        (shape((cols, m, n), BF16), shape((rows, m, n), BF16), shape((m, n), BF16)),
        3,
        [
            pltpu.VMEM((cols, n, n), BF16),
            pltpu.VMEM((rows, q, n, n), BF16),
            dma((1 + B, cols)),
            dma((2 * cols,)),
            dma((chips, rows)),
            dma((rows,)),
            dma((cols,)),
            dma((rows, q)),
        ],
        flops,
    )(left_basis, gradient, right_basis)
    rotated = call(
        functools.partial(second_kernel, rows, cols),
        1,
        shape((m, n), F32),
        2,
        [pltpu.VMEM((cols, m, n), BF16), dma((1 + B, cols)), dma((2 * cols,))],
        flops,
    )(left_rotated, rpanel)
    new_first = 0.9 * first_moment + 0.1 * rotated
    new_second = 0.95 * second_moment + 0.05 * rotated * rotated
    first_fix = 1.0 - 0.9**STEP
    second_fix = 1.0 - 0.95**STEP
    direction = (new_first / first_fix / (jnp.sqrt(new_second / second_fix) + 1e-08)).astype(BF16)
    parts = 2
    update = call(
        functools.partial(third_kernel, rows, cols, parts),
        2,
        shape((m, n), BF16),
        3,
        [
            pltpu.VMEM((rows, m, n), BF16),
            pltpu.VMEM((m, n), F32),
            pltpu.VMEM((m, n), BF16),
            pltpu.VMEM((B - 1, 2, LINE, m, n), BF16),
            pltpu.VMEM((LINE + 1, m, n), BF16),
            dma((chips, rows)),
            dma((rows,)),
            dma((B - 1, LINE, parts)),
            dma((B - 1, LINE, parts)),
            dma((LINE, parts)),
            dma((LINE + 1, parts)),
        ],
        2 * flops,
    )(direction, lpanel, rpanel)
    return (update, new_first, new_second)


def solution(mesh):
    spec = P("row", "col")
    return jax.shard_map(
        functools.partial(body, mesh.shape["row"], mesh.shape["col"]),
        mesh=mesh,
        in_specs=(spec,) * 5,
        out_specs=(spec,) * 3,
        check_vma=False,
    )
```
